32 devices in a mesh: groups: 2 (over y), expert: 16 (over z, x, core), dp: 1.
Axes of the slice: x: 2, y: 2, z: 4, core: 2. Of those that a mesh axis runs over, the one named last changes fastest.
Arguments:
- grad_out: bfloat16 [4096, 2048], P(('groups', 'expert', 'dp')), parts along dimension 0, may hold values from -6 to 6
- hidden: bfloat16 [4096, 8, 384], P(('groups', 'expert', 'dp')), parts along dimension 0, may hold values from -0.29882812 to 0.29882812
- routes: int32 [4096, 8], P(('groups', 'expert', 'dp')), parts along dimension 0, may hold values from 0 to 15, all different within a row; in each aligned block of 128 rows (0 to 127, 128 to 255, ...) at most 128 rows name the same one
- probs: bfloat16 [4096, 8], P(('groups', 'expert', 'dp')), parts along dimension 0, may hold values from 0.019897461 to 0.29882812
- w_down: bfloat16 [16, 384, 2048], P('expert', 'dp'), may hold values from -0.3125 to 0.3125
Outputs:
- grad_hidden: bfloat16 [4096, 8, 384], P(('groups', 'expert', 'dp')), parts along dimension 0
- grad_probs: bfloat16 [4096, 8], P(('groups', 'expert', 'dp')), parts along dimension 0
- grad_w: bfloat16 [32, 384, 2048], P(('groups', 'expert'), 'dp'), parts along dimension 0
The draws below stay inside these ranges and needn't reach their ends.
There are 2 independent parts, one for each index of `groups`. The reference program is written for one: setup_inputs(seed, part) draws one part's arguments, and reference() takes and returns one part's arrays. A program takes and returns all parts, laid end to end along the dimension named above; an argument that names none is the same for every part. Nothing has to cross between parts.
Inputs may be any that keep to these rules, and one draw needn't show every extreme that they name: `routes`: each token names 8 different experts. In each aligned block of 128 rows (the tokens of one device) no expert is named by more than 128 rows, a bound that some block reaches.
All inputs are finite; a program needn't handle non-finite values.
Results may differ from the reference program's by a relative error of at most 0.012.
Values may be sent and summed in bfloat16 or wider, within the bound.
No kernel may reach another device: no remote copies, remote signals or barrier semaphores. Data moves between devices by JAX's collectives and lax.ppermute only.
A program may use at most 64 MiB of HBM per device.

```python
import math
import jax
import jax.numpy as jnp
import numpy as np
from jax import lax

D = 2048
TOPK = 8
F = 384
TOK_DEV = 128
EXPERTS = 16
CAP = 128
TOKENS = 2048
N_EXPERT = 16
N_DP = 1


def block_levels(rng, extent, cuts, low, largest):
    def one(dim, parts):
        draws = jax.random.uniform(jax.random.fold_in(jax.random.fold_in(rng, 6), dim), (parts,), jnp.float32, low / len(cuts), largest / len(cuts))
        return jnp.repeat(jnp.exp(draws), extent[dim] // parts).reshape((-1,) + (1,) * (len(extent) - dim - 1))

    factor_of = one(*cuts[0])
    for cut in cuts[1:]:
        factor_of = factor_of * one(*cut)
    return factor_of


def routed_block(key, own, number, rows, amount, top, limit, lean):
    sequence = jax.random.permutation(key, amount)
    packed, ordinary = portions_of(amount, rows * top, limit, lean, True), portions_of(amount, rows * top, limit, lean, False)
    places = jnp.arange(amount)

    def named(tallies, offset_by):
        used = int((tallies > 0).sum())
        fixed = max(1, used // 4)
        shifted = fixed + (places - fixed + offset_by * (used - fixed)) % max(1, amount - fixed)
        return jnp.zeros((amount,), jnp.int32).at[sequence[jnp.where(places < fixed, places, shifted)]].set(jnp.asarray(tallies, jnp.int32))

    tallies = jnp.where(number % 4 == 0, named(packed, number // 4), named(ordinary, number - number // 4 - 1))
    mixed = jax.random.permutation(jax.random.fold_in(own, 3), amount)
    giver, taker = mixed[0:amount // 2 * 2:2], mixed[1:amount // 2 * 2:2]
    margin = jnp.minimum(tallies[giver] - 1, limit - tallies[taker]) // 2
    margin = jnp.where((giver == sequence[0]) | (taker == sequence[0]) | (tallies[taker] == 0), 0, jnp.maximum(margin, 0))
    shifted = jax.random.randint(jax.random.fold_in(own, 4), (amount // 2,), 0, 1 << 20) % (margin + 1)
    tallies = tallies.at[giver].add(-shifted).at[taker].add(shifted)
    labels = jnp.searchsorted(jnp.cumsum(tallies), jnp.arange(rows * top), side="right").astype(jnp.int32)
    table = labels.reshape(top, rows).T
    table = table[jax.random.permutation(jax.random.fold_in(own, 1), rows)]
    offset_by = jax.random.randint(jax.random.fold_in(own, 2), (rows, 1), 0, top)
    return jnp.take_along_axis(table, (jnp.arange(top)[None, :] + offset_by) % top, axis=1)


def portions_of(count, total, most, skew, full):
    weights = [(1 << 20) // math.isqrt(rank ** skew) + 1 for rank in range(1, count + 1)]
    largest = most if full else min(most, max(-(-total // count), total * weights[0] // sum(weights)))
    least = 1 if total - largest >= count - 1 else 0
    holding, surplus = [largest] + [least] * (count - 1), total - largest - least * (count - 1)
    while surplus > 0:
        movable = [i for i in range(1, count) if holding[i] < largest] or [i for i in range(1, count) if holding[i] < most]
        pool, left = sum([weights[i] for i in movable]), surplus
        for i in movable:
            addition = min(most - holding[i], max(1, left * weights[i] // pool), surplus)
            holding[i] = holding[i] + addition
            surplus = surplus - addition
    return np.array(holding)


def normal_values(key, dims, scale, reach, shards=(), kind=jnp.bfloat16):
    level = block_levels(key, dims, shards, -0.22, 0.18) if shards else 1.0
    array = jax.random.normal(key, dims, jnp.float32) * scale * level
    return jnp.minimum(jnp.maximum(array, -reach), reach).astype(kind)


def setup_inputs(seed: int = 0, part: int = 0) -> dict:
    streams_of = jax.random.split(jax.random.key(seed), 6)
    own_keys = jax.random.split(jax.random.fold_in(streams_of[5], part), 6)
    grad_out = normal_values(own_keys[0], (TOKENS, D), 1.0, 6.0, ((0, 16),))
    hidden = normal_values(own_keys[1], (TOKENS, TOPK, F), 0.05, 0.29882812, ((0, 16),))
    routes_keys = jax.random.split(jax.random.fold_in(own_keys[2], 1), TOKENS // TOK_DEV)
    routes_turns = jax.random.permutation(jax.random.fold_in(own_keys[2], 3), TOKENS // TOK_DEV)
    routes = jax.vmap(lambda own, number: routed_block(jax.random.fold_in(own_keys[2], 2), own, number, TOK_DEV, EXPERTS, TOPK, CAP, 2))(routes_keys, routes_turns).reshape((TOKENS, TOPK))
    probs = jnp.clip(0.019897461 + 0.27893066 * jax.random.uniform(own_keys[3], (TOKENS, TOPK), jnp.float32) ** block_levels(own_keys[3], (TOKENS, TOPK), ((0, 16),), -0.2, 0.2), 0.019897461, 0.29882812).astype(jnp.bfloat16)
    w_down = normal_values(streams_of[4], (EXPERTS, F, D), F ** -0.5, 0.3125, ((0, 16),))
    return {"grad_out": grad_out, "hidden": hidden, "routes": routes, "probs": probs, "w_down": w_down}


def reference(grad_out, hidden, routes, probs, w_down):
    token_count, top_count = routes.shape
    slot_count = token_count * top_count
    inner_width = hidden.shape[2]
    model_width = grad_out.shape[1]
    flat_ids = routes.reshape(slot_count).astype(jnp.int32)
    order = jnp.argsort(flat_ids, stable=True).astype(jnp.int32)
    loads = jnp.zeros((EXPERTS,), jnp.int32).at[flat_ids].add(1)
    starts = (jnp.cumsum(loads) - loads).astype(jnp.int32)
    longest = N_EXPERT * N_DP * CAP
    padded_order = jnp.concatenate([order, jnp.full((longest,), slot_count, jnp.int32)])
    grad_ext = jnp.concatenate([grad_out, jnp.zeros((1, model_width), grad_out.dtype)])
    hidden_ext = jnp.concatenate([hidden.reshape(slot_count, inner_width), jnp.zeros((1, inner_width), hidden.dtype)])
    probs_ext = jnp.concatenate([probs.reshape(slot_count), jnp.zeros((1,), probs.dtype)])

    def step(carry, expert_id):
        hidden_out, prob_out = carry
        chosen = lax.dynamic_slice(padded_order, (starts[expert_id],), (longest,))
        valid = jnp.arange(longest, dtype=jnp.int32) < loads[expert_id]
        chosen = jnp.where(valid, chosen, slot_count).astype(jnp.int32)
        token_index = jnp.where(valid, chosen // top_count, token_count).astype(jnp.int32)
        grad_rows = grad_ext[token_index]
        hidden_rows = hidden_ext[chosen]
        prob_rows = probs_ext[chosen].astype(jnp.float32)
        weight = w_down[expert_id]
        back_rows = jnp.dot(grad_rows, weight.T, preferred_element_type=jnp.float32)
        prob_grads = jnp.sum(back_rows * hidden_rows.astype(jnp.float32), axis=1).astype(jnp.bfloat16)
        hidden_grads = (prob_rows[:, None] * back_rows).astype(jnp.bfloat16)
        weighted = (grad_rows.astype(jnp.float32) * prob_rows[:, None]).astype(jnp.bfloat16)
        grad_weight = jnp.dot(hidden_rows.T, weighted, preferred_element_type=jnp.float32).astype(jnp.bfloat16)
        hidden_out = hidden_out.at[chosen].set(hidden_grads)
        prob_out = prob_out.at[chosen].set(prob_grads)
        return (hidden_out, prob_out), grad_weight

    start_carry = (jnp.zeros((slot_count + 1, inner_width), jnp.bfloat16), jnp.zeros((slot_count + 1,), jnp.bfloat16))
    (hidden_out, prob_out), grad_w = lax.scan(step, start_carry, jnp.arange(EXPERTS, dtype=jnp.int32))
    grad_hidden = hidden_out[:slot_count].reshape(token_count, top_count, inner_width)
    grad_probs = prob_out[:slot_count].reshape(token_count, top_count)
    return grad_hidden, grad_probs, grad_w
```

```python
import functools

import jax
import jax.numpy as jnp
import numpy as np
from jax import lax
from jax.experimental import pallas as pl
from jax.experimental.pallas import tpu as pltpu
from jax.sharding import PartitionSpec as P

GROUP = 16
VMEM = 48 * 1024 * 1024


def padded_on_device(grad_out, hidden, routes, probs, w_down):
    token_count, model_width = grad_out.shape
    top_count = routes.shape[1]
    inner_width = hidden.shape[2]
    peer_count = lax.axis_size("expert")
    capacity = min(token_count, max(2, 2 * token_count * top_count // peer_count))
    slot_count = token_count * top_count
    row_count = peer_count * capacity
    flat_ids = routes.reshape(slot_count)
    expert_row = jnp.arange(peer_count, dtype=jnp.int32)
    onehot = (flat_ids[:, None] == expert_row[None, :]).astype(jnp.int32)
    before = jnp.cumsum(onehot, axis=0) - onehot
    slot_rank = jnp.sum(before * onehot, axis=1)
    target = flat_ids * capacity + slot_rank
    slot_table = (
        jnp.full((row_count,), slot_count, jnp.int32)
        .at[target]
        .set(jnp.arange(slot_count, dtype=jnp.int32))
    )
    token_index = jnp.where(slot_table < slot_count, slot_table // top_count, token_count)
    grad_ext = jnp.concatenate([grad_out, jnp.zeros((1, model_width), grad_out.dtype)])
    hidden_ext = jnp.concatenate(
        [hidden.reshape(slot_count, inner_width), jnp.zeros((1, inner_width), hidden.dtype)]
    )
    probs_ext = jnp.concatenate([probs.reshape(slot_count), jnp.zeros((1,), probs.dtype)])
    send_grad = grad_ext[token_index].reshape(peer_count, capacity, model_width)
    send_hidden = hidden_ext[slot_table].reshape(peer_count, capacity, inner_width)
    send_probs = probs_ext[slot_table].reshape(peer_count, capacity)
    local_weight = w_down[0]
    half_width = local_weight.shape[0]
    got_grad, got_hidden, got_probs = (
        lax.all_to_all(send_grad, "expert", split_axis=0, concat_axis=0, tiled=True),
        lax.all_to_all(send_hidden, "expert", split_axis=0, concat_axis=0, tiled=True),
        lax.all_to_all(send_probs, "expert", split_axis=0, concat_axis=0, tiled=True),
    )
    grad_rows = got_grad.reshape(row_count, model_width)
    hidden_rows = got_hidden.reshape(row_count, inner_width)
    prob_rows = got_probs.reshape(row_count)
    back_rows = lax.dot_general(
        grad_rows,
        lax.all_gather(local_weight, "dp", axis=0, tiled=True),
        (((1,), (1,)), ((), ())),
        preferred_element_type=jnp.float32,
    )
    prob_grads = jnp.sum(back_rows * hidden_rows.astype(jnp.float32), axis=1).astype(jnp.bfloat16)
    hidden_grads = (prob_rows.astype(jnp.float32)[:, None] * back_rows).astype(jnp.bfloat16)
    weighted = grad_rows * prob_rows[:, None]
    returned_hidden, returned_probs = (
        lax.all_to_all(
            hidden_grads.reshape(peer_count, capacity, inner_width),
            "expert",
            split_axis=0,
            concat_axis=0,
            tiled=True,
        ),
        lax.all_to_all(
            prob_grads.reshape(peer_count, capacity),
            "expert",
            split_axis=0,
            concat_axis=0,
            tiled=True,
        ),
    )
    summed = lax.psum_scatter(
        lax.dot_general(
            hidden_rows, weighted, (((0,), (0,)), ((), ())), preferred_element_type=jnp.float32
        ).astype(jnp.bfloat16),
        "dp",
        scatter_dimension=0,
        tiled=True,
    )
    grad_w = summed.reshape(1, half_width, model_width)
    grad_hidden = returned_hidden.reshape(row_count, inner_width)[target].reshape(
        token_count, top_count, inner_width
    )
    grad_probs = returned_probs.reshape(row_count)[target].reshape(token_count, top_count)
    return (grad_hidden, grad_probs, grad_w)


def chosen_slots(route_row, expert_count, top_count):
    shape = (expert_count * GROUP, GROUP * top_count)
    row = lax.broadcasted_iota(jnp.int32, shape, 0)
    col = lax.broadcasted_iota(jnp.int32, shape, 1)
    return (row % GROUP == col // top_count) & (row // GROUP == route_row)


def dispatch_kernel(routes_ref, probs_ref, hidden_ref, out_ref, *, expert_count, top_count):
    span = GROUP * top_count
    inner_width = hidden_ref.shape[1]
    for g in range(routes_ref.shape[0]):
        chosen = chosen_slots(routes_ref[g : g + 1, :], expert_count, top_count)
        pick = jnp.where(chosen, probs_ref[g : g + 1, :].astype(jnp.float32), 0.0)
        rows = jnp.dot(
            pick.astype(jnp.bfloat16),
            hidden_ref[g * span : (g + 1) * span, :],
            preferred_element_type=jnp.float32,
        ).astype(jnp.bfloat16)
        out_ref[:, g * GROUP : (g + 1) * GROUP, :] = rows.reshape(expert_count, GROUP, inner_width)


def combine_kernel(
    routes_ref, probs_ref, hidden_ref, back_ref, hid_ref, prob_ref, *, expert_count, top_count
):
    span = GROUP * top_count
    inner_width = hidden_ref.shape[1]
    ones = jnp.ones((8, inner_width), jnp.bfloat16)
    across = (((0,), (0,)), ((), ()))
    lanes = (((1,), (1,)), ((), ()))
    for g in range(routes_ref.shape[0]):
        chosen = chosen_slots(routes_ref[g : g + 1, :], expert_count, top_count)
        pick = jnp.where(chosen, 1.0, 0.0).astype(jnp.bfloat16)
        scaled = jnp.where(chosen, probs_ref[g : g + 1, :].astype(jnp.float32), 0.0)
        block = back_ref[:, g * GROUP : (g + 1) * GROUP, :].reshape(expert_count * GROUP, inner_width)
        mine = lax.dot_general(pick, block, across, preferred_element_type=jnp.float32)
        hid_ref[g * span : (g + 1) * span, :] = lax.dot_general(
            scaled.astype(jnp.bfloat16), block, across, preferred_element_type=jnp.float32
        ).astype(jnp.bfloat16)
        product = mine * hidden_ref[g * span : (g + 1) * span, :].astype(jnp.float32)
        high = product.astype(jnp.bfloat16)
        low = (product - high.astype(jnp.float32)).astype(jnp.bfloat16)
        total = lax.dot_general(ones, high, lanes, preferred_element_type=jnp.float32)
        total += lax.dot_general(ones, low, lanes, preferred_element_type=jnp.float32)
        prob_ref[g : g + 1, :] = total[0:1, :].astype(jnp.bfloat16)


def back_kernel(ids_ref, *refs, places, step):
    pieces, (w_ref, out_ref, held, sems) = refs[: len(places)], refs[len(places) :]
    copies = []
    for i, (first, rows) in enumerate(places):
        copies.append(
            pltpu.make_async_copy(pieces[i], held.at[pl.ds(first, rows)], sems.at[i])
        )
        copies[i].start()
    block = out_ref.shape[1]
    waited = 0
    for first in range(0, held.shape[0], step):
        while waited < len(places) and places[waited][0] < first + step:
            copies[waited].wait()
            waited += 1
        rows = lax.dot_general(
            held[first : first + step, :],
            w_ref[...],
            (((1,), (1,)), ((), ())),
            preferred_element_type=jnp.float32,
        ).astype(jnp.bfloat16)
        for j in range(step // block):
            out_ref[ids_ref[first // block + j]] = rows[j * block : (j + 1) * block, :]


def weight_kernel(ids_ref, *refs, places, tile):
    pieces, (hidden_ref, out_ref, held, rows_held, sems, row_sems) = (
        refs[: len(places)],
        refs[len(places) :],
    )
    block = hidden_ref.shape[1]
    copies = []
    for j in range(hidden_ref.shape[0]):
        copies.append(
            pltpu.make_async_copy(
                hidden_ref.at[ids_ref[j]], rows_held.at[pl.ds(j * block, block)], row_sems.at[j]
            )
        )
    for i, (first, rows) in enumerate(places):
        copies.append(
            pltpu.make_async_copy(pieces[i], held.at[pl.ds(first, rows)], sems.at[i])
        )
    for copy in copies:
        copy.start()
    for copy in copies:
        copy.wait()

    @pl.loop(0, out_ref.shape[1] // tile)
    def _(n):
        cols = pl.ds(pl.multiple_of(n * tile, tile), tile)
        out_ref[:, cols] = lax.dot_general(
            rows_held[...],
            held[:, cols],
            (((0,), (0,)), ((), ())),
            preferred_element_type=jnp.float32,
        ).astype(jnp.bfloat16)


def ring_of_chips(chip_count):
    return list(range(0, chip_count, 2)) + list(range(chip_count - 1, 0, -2))


def gather_round(grad_out, peer_count):
    token_count = grad_out.shape[0]
    half = token_count // 2
    chips = peer_count // 2
    ring = ring_of_chips(chips)
    place = {chip: i for i, chip in enumerate(ring)}
    ahead = [
        (2 * chip + core, 2 * ring[(place[chip] + 1) % chips] + core)
        for chip in range(chips)
        for core in range(2)
    ]
    behind = [(b, a) for a, b in ahead]
    swap = [(i, i ^ 1) for i in range(peer_count)]
    offsets, own_core = [0], []
    own_core.append([(grad_out, 0, token_count)])
    fore = aft = grad_out
    for s in range(1, chips // 2):
        fore = lax.ppermute(fore, "expert", ahead)
        aft = lax.ppermute(aft, "expert", behind)
        own_core += [[(fore, 0, token_count)], [(aft, 0, token_count)]]
        offsets += [-s, s]
    own_core.append(
        [
            (lax.ppermute(fore[:half], "expert", ahead), 0, half),
            (lax.ppermute(aft[half:], "expert", behind), half, half),
        ]
    )
    offsets.append(chips // 2)
    pieces, places = [], []
    table = np.zeros((peer_count, peer_count), np.int32)
    for i, parts in enumerate(own_core):
        for j in range(2):
            for array, first, rows in parts:
                pieces.append(lax.ppermute(array, "expert", swap) if j else array)
                places.append(((2 * i + j) * token_count + first, rows))
        for peer in range(peer_count):
            chip, core = peer // 2, peer % 2
            source = ring[(place[chip] + offsets[i]) % chips]
            table[peer, 2 * i] = 2 * source + core
            table[peer, 2 * i + 1] = 2 * source + 1 - core
    ids = lax.dynamic_index_in_dim(
        jnp.asarray(table), lax.axis_index("expert"), 0, keepdims=False
    )
    return pieces, places, ids


def dense_on_device(grad_out, hidden, routes, probs, w_down):
    token_count, model_width = grad_out.shape
    top_count = routes.shape[1]
    inner_width = hidden.shape[2]
    peer_count = lax.axis_size("expert")
    slot_count = token_count * top_count
    row_count = peer_count * token_count
    span = GROUP * top_count
    route_rows = routes.reshape(slot_count // span, span)
    prob_rows = probs.reshape(slot_count // span, span)
    hidden_rows = hidden.reshape(slot_count, inner_width)
    local_weight = w_down[0]
    sizes = dict(expert_count=peer_count, top_count=top_count)
    params = pltpu.CompilerParams(vmem_limit_bytes=VMEM)
    anywhere = pl.BlockSpec(memory_space=pl.ANY)
    whole = pl.BlockSpec(memory_space=pltpu.VMEM)

    pieces, places, ids = gather_round(grad_out, peer_count)

    sent_hidden = pl.pallas_call(
        functools.partial(dispatch_kernel, **sizes),
        out_shape=jax.ShapeDtypeStruct((peer_count, token_count, inner_width), jnp.bfloat16),
        in_specs=[whole] * 3,
        out_specs=whole,
        compiler_params=params,
        name="dispatch",
    )(route_rows, prob_rows, hidden_rows)
    got_hidden = lax.all_to_all(sent_hidden, "expert", split_axis=0, concat_axis=0, tiled=True)

    back = pl.pallas_call(
        functools.partial(back_kernel, places=places, step=4 * token_count),
        out_shape=jax.ShapeDtypeStruct((peer_count, token_count, inner_width), jnp.bfloat16),
        in_specs=[pl.BlockSpec(memory_space=pltpu.SMEM)] + [anywhere] * len(pieces) + [whole],
        out_specs=whole,
        scratch_shapes=[
            pltpu.VMEM((row_count, model_width), jnp.bfloat16),
            pltpu.SemaphoreType.DMA((len(pieces),)),
        ],
        compiler_params=params,
        name="back_rows",
    )(ids, *pieces, local_weight)
    got_back = lax.all_to_all(back, "expert", split_axis=0, concat_axis=0, tiled=True)

    grad_w = pl.pallas_call(
        functools.partial(weight_kernel, places=places, tile=512),
        out_shape=jax.ShapeDtypeStruct((inner_width, model_width), jnp.bfloat16),
        in_specs=[pl.BlockSpec(memory_space=pltpu.SMEM)] + [anywhere] * (len(pieces) + 1),
        out_specs=whole,
        scratch_shapes=[
            pltpu.VMEM((row_count, model_width), jnp.bfloat16),
            pltpu.VMEM((row_count, inner_width), jnp.bfloat16),
            pltpu.SemaphoreType.DMA((len(pieces),)),
            pltpu.SemaphoreType.DMA((peer_count,)),
        ],
        compiler_params=params,
        name="grad_w",
    )(ids, *pieces, got_hidden)

    grad_hidden, grad_probs = pl.pallas_call(
        functools.partial(combine_kernel, **sizes),
        out_shape=(
            jax.ShapeDtypeStruct((slot_count, inner_width), jnp.bfloat16),
            jax.ShapeDtypeStruct((slot_count // span, span), jnp.bfloat16),
        ),
        in_specs=[whole] * 4,
        out_specs=(whole, whole),
        compiler_params=params,
        name="combine",
    )(route_rows, prob_rows, hidden_rows, got_back)
    return (
        grad_hidden.reshape(token_count, top_count, inner_width),
        grad_probs.reshape(token_count, top_count),
        grad_w[None],
    )


def on_device(grad_out, hidden, routes, probs, w_down):
    token_count = grad_out.shape[0]
    top_count = routes.shape[1]
    peer_count = lax.axis_size("expert")
    dense = (
        2 * top_count >= peer_count
        and lax.axis_size("dp") == 1
        and peer_count % 4 == 0
        and token_count % (2 * GROUP) == 0
        and (GROUP * top_count) % 128 == 0
    )
    body = dense_on_device if dense else padded_on_device
    return body(grad_out, hidden, routes, probs, w_down)


def solution(mesh):
    in_specs = (
        P(("groups", "expert", "dp"), None),
        P(("groups", "expert", "dp"), None, None),
        P(("groups", "expert", "dp"), None),
        P(("groups", "expert", "dp"), None),
        P("expert", "dp", None),
    )
    out_specs = (
        P(("groups", "expert", "dp"), None, None),
        P(("groups", "expert", "dp"), None),
        P(("groups", "expert"), "dp", None),
    )
    return jax.shard_map(
        on_device, mesh=mesh, in_specs=in_specs, out_specs=out_specs, check_vma=False
    )
```

```python
import functools

import jax
import jax.numpy as jnp
import numpy as np
from jax import lax
from jax.experimental import pallas as pl
from jax.experimental.pallas import tpu as pltpu
from jax.sharding import PartitionSpec as P

GROUP = 16
VMEM = 60 * 1024 * 1024
SMALL = 12 * 1024 * 1024


def padded_on_device(grad_out, hidden, routes, probs, w_down):
    token_count, model_width = grad_out.shape
    top_count = routes.shape[1]
    inner_width = hidden.shape[2]
    peer_count = lax.axis_size("expert")
    capacity = min(token_count, max(2, 2 * token_count * top_count // peer_count))
    slot_count = token_count * top_count
    row_count = peer_count * capacity
    flat_ids = routes.reshape(slot_count)
    expert_row = jnp.arange(peer_count, dtype=jnp.int32)
    onehot = (flat_ids[:, None] == expert_row[None, :]).astype(jnp.int32)
    before = jnp.cumsum(onehot, axis=0) - onehot
    slot_rank = jnp.sum(before * onehot, axis=1)
    target = flat_ids * capacity + slot_rank
    slot_table = (
        jnp.full((row_count,), slot_count, jnp.int32)
        .at[target]
        .set(jnp.arange(slot_count, dtype=jnp.int32))
    )
    token_index = jnp.where(slot_table < slot_count, slot_table // top_count, token_count)
    grad_ext = jnp.concatenate([grad_out, jnp.zeros((1, model_width), grad_out.dtype)])
    hidden_ext = jnp.concatenate(
        [hidden.reshape(slot_count, inner_width), jnp.zeros((1, inner_width), hidden.dtype)]
    )
    probs_ext = jnp.concatenate([probs.reshape(slot_count), jnp.zeros((1,), probs.dtype)])
    send_grad = grad_ext[token_index].reshape(peer_count, capacity, model_width)
    send_hidden = hidden_ext[slot_table].reshape(peer_count, capacity, inner_width)
    send_probs = probs_ext[slot_table].reshape(peer_count, capacity)
    local_weight = w_down[0]
    half_width = local_weight.shape[0]
    got_grad, got_hidden, got_probs = (
        lax.all_to_all(send_grad, "expert", split_axis=0, concat_axis=0, tiled=True),
        lax.all_to_all(send_hidden, "expert", split_axis=0, concat_axis=0, tiled=True),
        lax.all_to_all(send_probs, "expert", split_axis=0, concat_axis=0, tiled=True),
    )
    grad_rows = got_grad.reshape(row_count, model_width)
    hidden_rows = got_hidden.reshape(row_count, inner_width)
    prob_rows = got_probs.reshape(row_count)
    back_rows = lax.dot_general(
        grad_rows,
        lax.all_gather(local_weight, "dp", axis=0, tiled=True),
        (((1,), (1,)), ((), ())),
        preferred_element_type=jnp.float32,
    )
    prob_grads = jnp.sum(back_rows * hidden_rows.astype(jnp.float32), axis=1).astype(jnp.bfloat16)
    hidden_grads = (prob_rows.astype(jnp.float32)[:, None] * back_rows).astype(jnp.bfloat16)
    weighted = grad_rows * prob_rows[:, None]
    returned_hidden, returned_probs = (
        lax.all_to_all(
            hidden_grads.reshape(peer_count, capacity, inner_width),
            "expert",
            split_axis=0,
            concat_axis=0,
            tiled=True,
        ),
        lax.all_to_all(
            prob_grads.reshape(peer_count, capacity),
            "expert",
            split_axis=0,
            concat_axis=0,
            tiled=True,
        ),
    )
    summed = lax.psum_scatter(
        lax.dot_general(
            hidden_rows, weighted, (((0,), (0,)), ((), ())), preferred_element_type=jnp.float32
        ).astype(jnp.bfloat16),
        "dp",
        scatter_dimension=0,
        tiled=True,
    )
    grad_w = summed.reshape(1, half_width, model_width)
    grad_hidden = returned_hidden.reshape(row_count, inner_width)[target].reshape(
        token_count, top_count, inner_width
    )
    grad_probs = returned_probs.reshape(row_count)[target].reshape(token_count, top_count)
    return (grad_hidden, grad_probs, grad_w)


def chosen_slots(route_row, expert_count, top_count):
    shape = (expert_count * GROUP, GROUP * top_count)
    row = lax.broadcasted_iota(jnp.int32, shape, 0)
    col = lax.broadcasted_iota(jnp.int32, shape, 1)
    return (row % GROUP == col // top_count) & (row // GROUP == route_row)


def dispatch_kernel(routes_ref, probs_ref, hidden_ref, out_ref, *, expert_count, top_count):
    span = GROUP * top_count
    inner_width = hidden_ref.shape[1]
    for g in range(routes_ref.shape[0]):
        chosen = chosen_slots(routes_ref[g : g + 1, :], expert_count, top_count)
        pick = jnp.where(chosen, probs_ref[g : g + 1, :].astype(jnp.float32), 0.0)
        rows = jnp.dot(
            pick.astype(jnp.bfloat16),
            hidden_ref[g * span : (g + 1) * span, :],
            preferred_element_type=jnp.float32,
        ).astype(jnp.bfloat16)
        out_ref[:, g * GROUP : (g + 1) * GROUP, :] = rows.reshape(expert_count, GROUP, inner_width)


def combine_kernel(
    routes_ref, probs_ref, hidden_ref, back_ref, hid_ref, prob_ref, *, expert_count, top_count
):
    span = GROUP * top_count
    inner_width = hidden_ref.shape[1]
    ones = jnp.ones((top_count, inner_width), jnp.bfloat16)
    summed = jnp.zeros(prob_ref.shape, jnp.float32)
    row = lax.broadcasted_iota(jnp.int32, (top_count, span), 0)
    col = lax.broadcasted_iota(jnp.int32, (top_count, span), 1)
    slot = lax.broadcasted_iota(jnp.int32, (span, prob_ref.shape[1]), 0)
    token = lax.broadcasted_iota(jnp.int32, (span, prob_ref.shape[1]), 1)
    across = (((0,), (0,)), ((), ()))
    lanes = (((1,), (1,)), ((), ()))
    for g in range(routes_ref.shape[0]):
        chosen = chosen_slots(routes_ref[g : g + 1, :], expert_count, top_count)
        pick = jnp.where(chosen, 1.0, 0.0).astype(jnp.bfloat16)
        scaled = jnp.where(chosen, probs_ref[g : g + 1, :].astype(jnp.float32), 0.0)
        block = back_ref[:, g * GROUP : (g + 1) * GROUP, :].reshape(expert_count * GROUP, inner_width)
        mine = lax.dot_general(pick, block, across, preferred_element_type=jnp.float32)
        hid_ref[g * span : (g + 1) * span, :] = lax.dot_general(
            scaled.astype(jnp.bfloat16), block, across, preferred_element_type=jnp.float32
        ).astype(jnp.bfloat16)
        product = mine * hidden_ref[g * span : (g + 1) * span, :].astype(jnp.float32)
        high = product.astype(jnp.bfloat16)
        low = (product - high.astype(jnp.float32)).astype(jnp.bfloat16)
        total = lax.dot_general(ones, high, lanes, preferred_element_type=jnp.float32)
        total += lax.dot_general(ones, low, lanes, preferred_element_type=jnp.float32)
        own = jnp.where(col % top_count == row, total, 0.0).astype(jnp.bfloat16)
        to_token = jnp.where(token == slot // top_count + g * GROUP, 1.0, 0.0)
        summed += jnp.dot(own, to_token.astype(jnp.bfloat16), preferred_element_type=jnp.float32)
    prob_ref[...] = summed.astype(jnp.bfloat16)


def back_kernel(ids_ref, *refs, places, step):
    pieces, (w_ref, out_ref, held, sems) = refs[: len(places)], refs[len(places) :]
    copies = []
    for i, (first, rows) in enumerate(places):
        copies.append(
            pltpu.make_async_copy(pieces[i], held.at[pl.ds(first, rows)], sems.at[i])
        )
        copies[i].start()
    block = out_ref.shape[1]
    waited = 0
    for first in range(0, held.shape[0], step):
        while waited < len(places) and places[waited][0] < first + step:
            copies[waited].wait()
            waited += 1
        rows = lax.dot_general(
            held[first : first + step, :],
            w_ref[...],
            (((1,), (1,)), ((), ())),
            preferred_element_type=jnp.float32,
        ).astype(jnp.bfloat16)
        for j in range(step // block):
            out_ref[ids_ref[first // block + j]] = rows[j * block : (j + 1) * block, :]


def weight_kernel(ids_ref, *refs, places, tile):
    pieces, (hidden_ref, out_ref, held, rows_held, sems, row_sems) = (
        refs[: len(places)],
        refs[len(places) :],
    )
    block = hidden_ref.shape[1]
    copies = []
    for j in range(hidden_ref.shape[0]):
        copies.append(
            pltpu.make_async_copy(
                hidden_ref.at[ids_ref[j]], rows_held.at[pl.ds(j * block, block)], row_sems.at[j]
            )
        )
    for i, (first, rows) in enumerate(places):
        copies.append(
            pltpu.make_async_copy(pieces[i], held.at[pl.ds(first, rows)], sems.at[i])
        )
    for copy in copies:
        copy.start()
    for copy in copies:
        copy.wait()

    @pl.loop(0, out_ref.shape[1] // tile)
    def _(n):
        cols = pl.ds(pl.multiple_of(n * tile, tile), tile)
        out_ref[:, cols] = lax.dot_general(
            rows_held[...],
            held[:, cols],
            (((0,), (0,)), ((), ())),
            preferred_element_type=jnp.float32,
        ).astype(jnp.bfloat16)


def ring_of_chips(chip_count):
    return list(range(0, chip_count, 2)) + list(range(chip_count - 1, 0, -2))


def gather_round(grad_out, peer_count):
    token_count = grad_out.shape[0]
    half = token_count // 2
    chips = peer_count // 2
    ring = ring_of_chips(chips)
    place = {chip: i for i, chip in enumerate(ring)}
    ahead = [
        (2 * chip + core, 2 * ring[(place[chip] + 1) % chips] + core)
        for chip in range(chips)
        for core in range(2)
    ]
    behind = [(b, a) for a, b in ahead]
    swap = [(i, i ^ 1) for i in range(peer_count)]
    offsets, own_core = [0], []
    own_core.append([(grad_out, 0, token_count)])
    fore = aft = grad_out
    for s in range(1, chips // 2):
        fore = lax.ppermute(fore, "expert", ahead)
        aft = lax.ppermute(aft, "expert", behind)
        own_core += [[(fore, 0, token_count)], [(aft, 0, token_count)]]
        offsets += [-s, s]
    late = (
        lax.ppermute(fore[:half], "expert", ahead),
        lax.ppermute(aft[half:], "expert", behind),
    )
    own_core.append([(late[0], 0, half), (late[1], half, half)])
    offsets.append(chips // 2)
    pieces, places = [], []
    table = np.zeros((peer_count, peer_count), np.int32)
    for i, parts in enumerate(own_core):
        for j in range(2):
            for array, first, rows in parts:
                pieces.append(lax.ppermute(array, "expert", swap) if j else array)
                places.append(((2 * i + j) * token_count + first, rows))
        for peer in range(peer_count):
            chip, core = peer // 2, peer % 2
            source = ring[(place[chip] + offsets[i]) % chips]
            table[peer, 2 * i] = 2 * source + core
            table[peer, 2 * i + 1] = 2 * source + 1 - core
    ids = lax.dynamic_index_in_dim(
        jnp.asarray(table), lax.axis_index("expert"), 0, keepdims=False
    )
    return pieces, places, ids, late


def dense_on_device(grad_out, hidden, routes, probs, w_down):
    token_count, model_width = grad_out.shape
    top_count = routes.shape[1]
    inner_width = hidden.shape[2]
    peer_count = lax.axis_size("expert")
    slot_count = token_count * top_count
    row_count = peer_count * token_count
    span = GROUP * top_count
    route_rows = routes.reshape(slot_count // span, span)
    prob_rows = probs.reshape(slot_count // span, span)
    hidden_rows = hidden.reshape(slot_count, inner_width)
    local_weight = w_down[0]
    sizes = dict(expert_count=peer_count, top_count=top_count)
    params = pltpu.CompilerParams(vmem_limit_bytes=VMEM)
    small = pltpu.CompilerParams(vmem_limit_bytes=SMALL)
    anywhere = pl.BlockSpec(memory_space=pltpu.HBM)
    whole = pl.BlockSpec(memory_space=pltpu.VMEM)

    pieces, places, ids, late = gather_round(grad_out, peer_count)

    sent_hidden = pl.pallas_call(
        functools.partial(dispatch_kernel, **sizes),
        out_shape=jax.ShapeDtypeStruct((peer_count, token_count, inner_width), jnp.bfloat16),
        in_specs=[whole] * 3,
        out_specs=whole,
        compiler_params=small,
        name="dispatch",
    )(route_rows, prob_rows, hidden_rows)
    sent_hidden, *_ = lax.optimization_barrier((sent_hidden, *late))
    got_hidden = lax.all_to_all(sent_hidden, "expert", split_axis=0, concat_axis=0, tiled=True)

    back = pl.pallas_call(
        functools.partial(back_kernel, places=places, step=4 * token_count),
        out_shape=jax.ShapeDtypeStruct((peer_count, token_count, inner_width), jnp.bfloat16),
        in_specs=[pl.BlockSpec(memory_space=pltpu.SMEM)] + [anywhere] * len(pieces) + [whole],
        out_specs=whole,
        scratch_shapes=[
            pltpu.VMEM((row_count, model_width), jnp.bfloat16),
            pltpu.SemaphoreType.DMA((len(pieces),)),
        ],
        compiler_params=params,
        name="back_rows",
    )(ids, *pieces, local_weight)
    got_back = lax.all_to_all(back, "expert", split_axis=0, concat_axis=0, tiled=True)

    grad_w = pl.pallas_call(
        functools.partial(weight_kernel, places=places, tile=512),
        out_shape=jax.ShapeDtypeStruct((inner_width, model_width), jnp.bfloat16),
        in_specs=[pl.BlockSpec(memory_space=pltpu.SMEM)] + [anywhere] * (len(pieces) + 1),
        out_specs=whole,
        scratch_shapes=[
            pltpu.VMEM((row_count, model_width), jnp.bfloat16),
            pltpu.VMEM((row_count, inner_width), jnp.bfloat16),
            pltpu.SemaphoreType.DMA((len(pieces),)),
            pltpu.SemaphoreType.DMA((peer_count,)),
        ],
        compiler_params=params,
        name="grad_w",
    )(ids, *pieces, got_hidden)

    grad_hidden, grad_probs = pl.pallas_call(
        functools.partial(combine_kernel, **sizes),
        out_shape=(
            jax.ShapeDtypeStruct((slot_count, inner_width), jnp.bfloat16),
            jax.ShapeDtypeStruct((top_count, token_count), jnp.bfloat16),
        ),
        in_specs=[whole] * 4,
        out_specs=(whole, whole),
        compiler_params=small,
        name="combine",
    )(route_rows, prob_rows, hidden_rows, got_back)
    return (
        grad_hidden.reshape(token_count, top_count, inner_width),
        grad_probs.T,
        grad_w[None],
    )


def on_device(grad_out, hidden, routes, probs, w_down):
    token_count = grad_out.shape[0]
    top_count = routes.shape[1]
    peer_count = lax.axis_size("expert")
    dense = (
        2 * top_count >= peer_count
        and lax.axis_size("dp") == 1
        and peer_count % 4 == 0
        and token_count % (2 * GROUP) == 0
        and (GROUP * top_count) % 128 == 0
    )
    body = dense_on_device if dense else padded_on_device
    return body(grad_out, hidden, routes, probs, w_down)


def solution(mesh):
    in_specs = (
        P(("groups", "expert", "dp"), None),
        P(("groups", "expert", "dp"), None, None),
        P(("groups", "expert", "dp"), None),
        P(("groups", "expert", "dp"), None),
        P("expert", "dp", None),
    )
    out_specs = (
        P(("groups", "expert", "dp"), None, None),
        P(("groups", "expert", "dp"), None),
        P(("groups", "expert"), "dp", None),
    )
    return jax.shard_map(
        on_device, mesh=mesh, in_specs=in_specs, out_specs=out_specs, check_vma=False
    )
```

```python
import functools

import jax
import jax.numpy as jnp
import numpy as np
from jax import lax
from jax.experimental import pallas as pl
from jax.experimental.pallas import tpu as pltpu
from jax.sharding import PartitionSpec as P

TILE = 512
GROUP = 16
SPLIT = 1
VMEM = 60 * 1024 * 1024
SMALL = 12 * 1024 * 1024


def padded_on_device(grad_out, hidden, routes, probs, w_down):
    token_count, model_width = grad_out.shape
    top_count = routes.shape[1]
    inner_width = hidden.shape[2]
    peer_count = lax.axis_size("expert")
    capacity = min(token_count, max(2, 2 * token_count * top_count // peer_count))
    slot_count = token_count * top_count
    row_count = peer_count * capacity
    flat_ids = routes.reshape(slot_count)
    expert_row = jnp.arange(peer_count, dtype=jnp.int32)
    onehot = (flat_ids[:, None] == expert_row[None, :]).astype(jnp.int32)
    before = jnp.cumsum(onehot, axis=0) - onehot
    slot_rank = jnp.sum(before * onehot, axis=1)
    target = flat_ids * capacity + slot_rank
    slot_table = (
        jnp.full((row_count,), slot_count, jnp.int32)
        .at[target]
        .set(jnp.arange(slot_count, dtype=jnp.int32))
    )
    token_index = jnp.where(slot_table < slot_count, slot_table // top_count, token_count)
    grad_ext = jnp.concatenate([grad_out, jnp.zeros((1, model_width), grad_out.dtype)])
    hidden_ext = jnp.concatenate(
        [hidden.reshape(slot_count, inner_width), jnp.zeros((1, inner_width), hidden.dtype)]
    )
    probs_ext = jnp.concatenate([probs.reshape(slot_count), jnp.zeros((1,), probs.dtype)])
    send_grad = grad_ext[token_index].reshape(peer_count, capacity, model_width)
    send_hidden = hidden_ext[slot_table].reshape(peer_count, capacity, inner_width)
    send_probs = probs_ext[slot_table].reshape(peer_count, capacity)
    local_weight = w_down[0]
    half_width = local_weight.shape[0]
    got_grad, got_hidden, got_probs = (
        lax.all_to_all(send_grad, "expert", split_axis=0, concat_axis=0, tiled=True),
        lax.all_to_all(send_hidden, "expert", split_axis=0, concat_axis=0, tiled=True),
        lax.all_to_all(send_probs, "expert", split_axis=0, concat_axis=0, tiled=True),
    )
    grad_rows = got_grad.reshape(row_count, model_width)
    hidden_rows = got_hidden.reshape(row_count, inner_width)
    prob_rows = got_probs.reshape(row_count)
    back_rows = lax.dot_general(
        grad_rows,
        lax.all_gather(local_weight, "dp", axis=0, tiled=True),
        (((1,), (1,)), ((), ())),
        preferred_element_type=jnp.float32,
    )
    prob_grads = jnp.sum(back_rows * hidden_rows.astype(jnp.float32), axis=1).astype(jnp.bfloat16)
    hidden_grads = (prob_rows.astype(jnp.float32)[:, None] * back_rows).astype(jnp.bfloat16)
    weighted = grad_rows * prob_rows[:, None]
    returned_hidden, returned_probs = (
        lax.all_to_all(
            hidden_grads.reshape(peer_count, capacity, inner_width),
            "expert",
            split_axis=0,
            concat_axis=0,
            tiled=True,
        ),
        lax.all_to_all(
            prob_grads.reshape(peer_count, capacity),
            "expert",
            split_axis=0,
            concat_axis=0,
            tiled=True,
        ),
    )
    summed = lax.psum_scatter(
        lax.dot_general(
            hidden_rows, weighted, (((0,), (0,)), ((), ())), preferred_element_type=jnp.float32
        ).astype(jnp.bfloat16),
        "dp",
        scatter_dimension=0,
        tiled=True,
    )
    grad_w = summed.reshape(1, half_width, model_width)
    grad_hidden = returned_hidden.reshape(row_count, inner_width)[target].reshape(
        token_count, top_count, inner_width
    )
    grad_probs = returned_probs.reshape(row_count)[target].reshape(token_count, top_count)
    return (grad_hidden, grad_probs, grad_w)


def chosen_slots(route_row, expert_count, top_count):
    shape = (expert_count * GROUP, GROUP * top_count)
    row = lax.broadcasted_iota(jnp.int32, shape, 0)
    col = lax.broadcasted_iota(jnp.int32, shape, 1)
    return (row % GROUP == col // top_count) & (row // GROUP == route_row)


def dispatch_kernel(routes_ref, probs_ref, hidden_ref, out_ref, *, expert_count, top_count):
    span = GROUP * top_count
    inner_width = hidden_ref.shape[1]
    for g in range(routes_ref.shape[0]):
        chosen = chosen_slots(routes_ref[g : g + 1, :], expert_count, top_count)
        pick = jnp.where(chosen, probs_ref[g : g + 1, :].astype(jnp.float32), 0.0)
        rows = jnp.dot(
            pick.astype(jnp.bfloat16),
            hidden_ref[g * span : (g + 1) * span, :],
            preferred_element_type=jnp.float32,
        ).astype(jnp.bfloat16)
        out_ref[:, g * GROUP : (g + 1) * GROUP, :] = rows.reshape(expert_count, GROUP, inner_width)


def combine_kernel(routes_ref, probs_ref, hidden_ref, *refs, top_count):
    back_refs, (hid_ref, prob_ref) = refs[:-2], refs[-2:]
    span = GROUP * top_count
    inner_width = hidden_ref.shape[1]
    ones = jnp.ones((top_count, inner_width), jnp.bfloat16)
    summed = jnp.zeros(prob_ref.shape, jnp.float32)
    row = lax.broadcasted_iota(jnp.int32, (top_count, span), 0)
    col = lax.broadcasted_iota(jnp.int32, (top_count, span), 1)
    slot = lax.broadcasted_iota(jnp.int32, (span, prob_ref.shape[1]), 0)
    token = lax.broadcasted_iota(jnp.int32, (span, prob_ref.shape[1]), 1)
    across = (((0,), (0,)), ((), ()))
    lanes = (((1,), (1,)), ((), ()))
    for g in range(routes_ref.shape[0]):
        chosen = chosen_slots(routes_ref[g : g + 1, :], len(back_refs), top_count)
        pick = jnp.where(chosen, 1.0, 0.0).astype(jnp.bfloat16)
        scaled = jnp.where(chosen, probs_ref[g : g + 1, :].astype(jnp.float32), 0.0)
        block = jnp.concatenate(
            [ref[g * GROUP : (g + 1) * GROUP, :] for ref in back_refs], axis=0
        )
        mine = lax.dot_general(pick, block, across, preferred_element_type=jnp.float32)
        hid_ref[g * span : (g + 1) * span, :] = lax.dot_general(
            scaled.astype(jnp.bfloat16), block, across, preferred_element_type=jnp.float32
        ).astype(jnp.bfloat16)
        product = mine * hidden_ref[g * span : (g + 1) * span, :].astype(jnp.float32)
        high = product.astype(jnp.bfloat16)
        low = (product - high.astype(jnp.float32)).astype(jnp.bfloat16)
        total = lax.dot_general(ones, high, lanes, preferred_element_type=jnp.float32)
        total += lax.dot_general(ones, low, lanes, preferred_element_type=jnp.float32)
        own = jnp.where(col % top_count == row, total, 0.0).astype(jnp.bfloat16)
        to_token = jnp.where(token == slot // top_count + g * GROUP, 1.0, 0.0)
        summed += jnp.dot(own, to_token.astype(jnp.bfloat16), preferred_element_type=jnp.float32)
    prob_ref[...] = summed.astype(jnp.bfloat16)


def back_kernel(order_ref, *refs, places, step, block):
    pieces, w_ref = refs[: len(places)], refs[len(places)]
    out_refs, (held, rows_held, sems) = refs[len(places) + 1 : -3], refs[-3:]
    copies = []
    for i, (first, rows) in enumerate(places):
        copies.append(
            pltpu.make_async_copy(pieces[i], held.at[pl.ds(first, rows)], sems.at[i])
        )
        copies[i].start()
    waited = 0
    for first in range(0, held.shape[0], step):
        while waited < len(places) and places[waited][0] < first + step:
            copies[waited].wait()
            waited += 1
        rows = lax.dot_general(
            held[first : first + step, :],
            w_ref[...],
            (((1,), (1,)), ((), ())),
            preferred_element_type=jnp.float32,
        ).astype(jnp.bfloat16)
        for j in range(step // block):
            rows_held[first // block + j] = rows[j * block : (j + 1) * block, :]
    for k, out_ref in enumerate(out_refs):
        out_ref[...] = rows_held[order_ref[k]]


def weight_kernel(ids_ref, *refs, places, first_col):
    hidden_ref, out_ref, held, rows_held, sems, row_sems = refs[-6:]
    pieces = refs[: len(places)]
    block = hidden_ref.shape[1]
    cols = pl.ds(first_col, out_ref.shape[1])
    copies = []
    for j in range(hidden_ref.shape[0]):
        copies.append(
            pltpu.make_async_copy(
                hidden_ref.at[ids_ref[j]], rows_held.at[pl.ds(j * block, block)], row_sems.at[j]
            )
        )
    for i, (first, rows) in enumerate(places):
        copies.append(
            pltpu.make_async_copy(pieces[i].at[:, cols], held.at[pl.ds(first, rows)], sems.at[i])
        )
    for copy in copies:
        copy.start()
    for copy in copies:
        copy.wait()
    tile = min(TILE, out_ref.shape[1])

    @pl.loop(0, out_ref.shape[1] // tile)
    def _(n):
        part = pl.ds(pl.multiple_of(n * tile, tile), tile)
        out_ref[:, part] = lax.dot_general(
            rows_held[...],
            held[:, part],
            (((0,), (0,)), ((), ())),
            preferred_element_type=jnp.float32,
        ).astype(jnp.bfloat16)


def ring_of_chips(chip_count):
    return list(range(0, chip_count, 2)) + list(range(chip_count - 1, 0, -2))


def gather_round(grad_out, peer_count):
    token_count = grad_out.shape[0]
    half = token_count // 2
    chips = peer_count // 2
    ring = ring_of_chips(chips)
    place = {chip: i for i, chip in enumerate(ring)}
    ahead = [
        (2 * chip + core, 2 * ring[(place[chip] + 1) % chips] + core)
        for chip in range(chips)
        for core in range(2)
    ]
    behind = [(b, a) for a, b in ahead]
    swap = [(i, i ^ 1) for i in range(peer_count)]
    low, high = grad_out[:half], grad_out[half:]
    offsets, own_core = [0], [[(low, 0, half), (high, half, half)]]
    low_fore = low_aft = low
    high_fore = high_aft = high
    for s in range(1, chips // 2):
        low_fore = lax.ppermute(low_fore, "expert", ahead)
        high_aft = lax.ppermute(high_aft, "expert", behind)
        high_fore = lax.ppermute(high_fore, "expert", ahead)
        low_aft = lax.ppermute(low_aft, "expert", behind)
        own_core += [
            [(low_fore, 0, half), (high_fore, half, half)],
            [(low_aft, 0, half), (high_aft, half, half)],
        ]
        offsets += [-s, s]
    late = (
        lax.ppermute(low_fore, "expert", ahead),
        lax.ppermute(high_aft, "expert", behind),
        high_fore,
        low_aft,
    )
    own_core.append([(late[0], 0, half), (late[1], half, half)])
    offsets.append(chips // 2)
    pieces, places = [], []
    table = np.zeros((peer_count, peer_count), np.int32)
    for i, parts in enumerate(own_core):
        for j in range(2):
            for array, first, rows in parts:
                pieces.append(lax.ppermute(array, "expert", swap) if j else array)
                places.append(((2 * i + j) * token_count + first, rows))
        for peer in range(peer_count):
            chip, core = peer // 2, peer % 2
            source = ring[(place[chip] + offsets[i]) % chips]
            table[peer, 2 * i] = 2 * source + core
            table[peer, 2 * i + 1] = 2 * source + 1 - core
    return pieces, places, table, late


def exchange(blocks, some):
    peers = range(len(blocks))
    return {k: lax.ppermute(blocks[k], "expert", [(i, i ^ k) for i in peers]) for k in some}


def dense_on_device(grad_out, hidden, routes, probs, w_down):
    token_count, model_width = grad_out.shape
    top_count = routes.shape[1]
    inner_width = hidden.shape[2]
    peer_count = lax.axis_size("expert")
    slot_count = token_count * top_count
    row_count = peer_count * token_count
    span = GROUP * top_count
    me = lax.axis_index("expert")
    route_rows = routes.reshape(slot_count // span, span)
    prob_rows = probs.reshape(slot_count // span, span)
    hidden_rows = hidden.reshape(slot_count, inner_width)
    local_weight = w_down[0]
    params = pltpu.CompilerParams(vmem_limit_bytes=VMEM)
    small = pltpu.CompilerParams(vmem_limit_bytes=SMALL)
    scalars = pl.BlockSpec(memory_space=pltpu.SMEM)
    whole = pl.BlockSpec(memory_space=pltpu.VMEM)
    far = pl.BlockSpec(memory_space=pltpu.HBM)
    block = jax.ShapeDtypeStruct((token_count, inner_width), jnp.bfloat16)

    pieces, places, table, late = gather_round(grad_out, peer_count)
    ids = lax.dynamic_index_in_dim(jnp.asarray(table), me, 0, keepdims=False)
    order = np.stack([np.argsort(table[peer] ^ peer) for peer in range(peer_count)])
    order = lax.dynamic_index_in_dim(
        jnp.asarray(order.astype(np.int32)), me, 0, keepdims=False
    )

    sent = pl.pallas_call(
        functools.partial(dispatch_kernel, expert_count=peer_count, top_count=top_count),
        out_shape=jax.ShapeDtypeStruct((peer_count, token_count, inner_width), jnp.bfloat16),
        in_specs=[whole] * 3,
        out_specs=whole,
        compiler_params=small,
        name="dispatch",
    )(route_rows, prob_rows, hidden_rows)
    sent, _ = lax.optimization_barrier((sent, late))
    got_hidden = lax.all_to_all(sent, "expert", split_axis=0, concat_axis=0, tiled=True)

    back = pl.pallas_call(
        functools.partial(back_kernel, places=places, step=4 * token_count, block=token_count),
        out_shape=[block] * peer_count,
        in_specs=[scalars] + [far] * len(pieces) + [whole],
        out_specs=[whole] * peer_count,
        scratch_shapes=[
            pltpu.VMEM((row_count, model_width), jnp.bfloat16),
            pltpu.VMEM((peer_count, token_count, inner_width), jnp.bfloat16),
            pltpu.SemaphoreType.DMA((len(pieces),)),
        ],
        compiler_params=params,
        cost_estimate=pl.CostEstimate(
            flops=2 * row_count * inner_width * model_width,
            bytes_accessed=2 * (row_count + inner_width) * model_width,
            transcendentals=0,
        ),
        name="back_rows",
    )(order, *pieces, local_weight)
    held_back = range(peer_count - 3, peer_count)
    got_back = {0: back[0]} | exchange(back, [k for k in range(1, peer_count) if k not in held_back])

    near = {k: got_back[k] for k in range(1, peer_count // 2)}
    got_hidden, near = lax.optimization_barrier((got_hidden, near))
    got_back |= near
    width = model_width // SPLIT
    grad_w = [
        pl.pallas_call(
            functools.partial(weight_kernel, places=places, first_col=n * width),
            out_shape=jax.ShapeDtypeStruct((inner_width, width), jnp.bfloat16),
            in_specs=[scalars] + [far] * len(pieces) + [pl.BlockSpec(memory_space=pl.ANY)],
            out_specs=whole,
            scratch_shapes=[
                pltpu.VMEM((row_count, width), jnp.bfloat16),
                pltpu.VMEM((row_count, inner_width), jnp.bfloat16),
                pltpu.SemaphoreType.DMA((len(pieces),)),
                pltpu.SemaphoreType.DMA((peer_count,)),
            ],
            compiler_params=params,
            cost_estimate=pl.CostEstimate(
                flops=2 * row_count * inner_width * width,
                bytes_accessed=2 * (row_count * (width + inner_width) + inner_width * width),
                transcendentals=0,
            ),
            name="grad_w",
        )(ids, *pieces, got_hidden)
        for n in range(SPLIT)
    ]
    grad_w = jnp.concatenate(grad_w, axis=1) if SPLIT > 1 else grad_w[0]

    back, grad_w = lax.optimization_barrier((back, grad_w))
    got_back |= exchange(back, held_back)
    got_back = [got_back[k] for k in range(peer_count)]
    grad_hidden, grad_probs = pl.pallas_call(
        functools.partial(combine_kernel, top_count=top_count),
        out_shape=(
            jax.ShapeDtypeStruct((slot_count, inner_width), jnp.bfloat16),
            jax.ShapeDtypeStruct((top_count, token_count), jnp.bfloat16),
        ),
        in_specs=[whole] * (3 + peer_count),
        out_specs=(whole, whole),
        compiler_params=small,
        name="combine",
    )((routes ^ me).reshape(slot_count // span, span), prob_rows, hidden_rows, *got_back)
    return (
        grad_hidden.reshape(token_count, top_count, inner_width),
        grad_probs.T,
        grad_w[None],
    )


def on_device(grad_out, hidden, routes, probs, w_down):
    token_count = grad_out.shape[0]
    top_count = routes.shape[1]
    peer_count = lax.axis_size("expert")
    dense = (
        2 * top_count >= peer_count
        and lax.axis_size("dp") == 1
        and peer_count % 4 == 0
        and peer_count & (peer_count - 1) == 0
        and token_count % (2 * GROUP) == 0
        and (GROUP * top_count) % 128 == 0
    )
    body = dense_on_device if dense else padded_on_device
    return body(grad_out, hidden, routes, probs, w_down)


def solution(mesh):
    in_specs = (
        P(("groups", "expert", "dp"), None),
        P(("groups", "expert", "dp"), None, None),
        P(("groups", "expert", "dp"), None),
        P(("groups", "expert", "dp"), None),
        P("expert", "dp", None),
    )
    out_specs = (
        P(("groups", "expert", "dp"), None, None),
        P(("groups", "expert", "dp"), None),
        P(("groups", "expert"), "dp", None),
    )
    return jax.shard_map(
        on_device, mesh=mesh, in_specs=in_specs, out_specs=out_specs, check_vma=False
    )
```

```python
import functools

import jax
import jax.numpy as jnp
import numpy as np
from jax import lax
from jax.experimental import pallas as pl
from jax.experimental.pallas import tpu as pltpu
from jax.sharding import PartitionSpec as P

TILE = 512
GROUP = 16
SPLIT = 1
VMEM = 60 * 1024 * 1024
SMALL = 12 * 1024 * 1024


def padded_on_device(grad_out, hidden, routes, probs, w_down):
    token_count, model_width = grad_out.shape
    top_count = routes.shape[1]
    inner_width = hidden.shape[2]
    peer_count = lax.axis_size("expert")
    capacity = min(token_count, max(2, 2 * token_count * top_count // peer_count))
    slot_count = token_count * top_count
    row_count = peer_count * capacity
    flat_ids = routes.reshape(slot_count)
    expert_row = jnp.arange(peer_count, dtype=jnp.int32)
    onehot = (flat_ids[:, None] == expert_row[None, :]).astype(jnp.int32)
    before = jnp.cumsum(onehot, axis=0) - onehot
    slot_rank = jnp.sum(before * onehot, axis=1)
    target = flat_ids * capacity + slot_rank
    slot_table = (
        jnp.full((row_count,), slot_count, jnp.int32)
        .at[target]
        .set(jnp.arange(slot_count, dtype=jnp.int32))
    )
    token_index = jnp.where(slot_table < slot_count, slot_table // top_count, token_count)
    grad_ext = jnp.concatenate([grad_out, jnp.zeros((1, model_width), grad_out.dtype)])
    hidden_ext = jnp.concatenate(
        [hidden.reshape(slot_count, inner_width), jnp.zeros((1, inner_width), hidden.dtype)]
    )
    probs_ext = jnp.concatenate([probs.reshape(slot_count), jnp.zeros((1,), probs.dtype)])
    send_grad = grad_ext[token_index].reshape(peer_count, capacity, model_width)
    send_hidden = hidden_ext[slot_table].reshape(peer_count, capacity, inner_width)
    send_probs = probs_ext[slot_table].reshape(peer_count, capacity)
    local_weight = w_down[0]
    half_width = local_weight.shape[0]
    got_grad, got_hidden, got_probs = (
        lax.all_to_all(send_grad, "expert", split_axis=0, concat_axis=0, tiled=True),
        lax.all_to_all(send_hidden, "expert", split_axis=0, concat_axis=0, tiled=True),
        lax.all_to_all(send_probs, "expert", split_axis=0, concat_axis=0, tiled=True),
    )
    grad_rows = got_grad.reshape(row_count, model_width)
    hidden_rows = got_hidden.reshape(row_count, inner_width)
    prob_rows = got_probs.reshape(row_count)
    back_rows = lax.dot_general(
        grad_rows,
        lax.all_gather(local_weight, "dp", axis=0, tiled=True),
        (((1,), (1,)), ((), ())),
        preferred_element_type=jnp.float32,
    )
    prob_grads = jnp.sum(back_rows * hidden_rows.astype(jnp.float32), axis=1).astype(jnp.bfloat16)
    hidden_grads = (prob_rows.astype(jnp.float32)[:, None] * back_rows).astype(jnp.bfloat16)
    weighted = grad_rows * prob_rows[:, None]
    returned_hidden, returned_probs = (
        lax.all_to_all(
            hidden_grads.reshape(peer_count, capacity, inner_width),
            "expert",
            split_axis=0,
            concat_axis=0,
            tiled=True,
        ),
        lax.all_to_all(
            prob_grads.reshape(peer_count, capacity),
            "expert",
            split_axis=0,
            concat_axis=0,
            tiled=True,
        ),
    )
    summed = lax.psum_scatter(
        lax.dot_general(
            hidden_rows, weighted, (((0,), (0,)), ((), ())), preferred_element_type=jnp.float32
        ).astype(jnp.bfloat16),
        "dp",
        scatter_dimension=0,
        tiled=True,
    )
    grad_w = summed.reshape(1, half_width, model_width)
    grad_hidden = returned_hidden.reshape(row_count, inner_width)[target].reshape(
        token_count, top_count, inner_width
    )
    grad_probs = returned_probs.reshape(row_count)[target].reshape(token_count, top_count)
    return (grad_hidden, grad_probs, grad_w)


def chosen_slots(route_row, expert_count, top_count):
    shape = (expert_count * GROUP, GROUP * top_count)
    row = lax.broadcasted_iota(jnp.int32, shape, 0)
    col = lax.broadcasted_iota(jnp.int32, shape, 1)
    return (row % GROUP == col // top_count) & (row // GROUP == route_row)


def dispatch_kernel(routes_ref, probs_ref, hidden_ref, out_ref, *, expert_count, top_count):
    span = GROUP * top_count
    inner_width = hidden_ref.shape[1]
    for g in range(routes_ref.shape[0]):
        chosen = chosen_slots(routes_ref[g : g + 1, :], expert_count, top_count)
        pick = jnp.where(chosen, probs_ref[g : g + 1, :].astype(jnp.float32), 0.0)
        rows = jnp.dot(
            pick.astype(jnp.bfloat16),
            hidden_ref[g * span : (g + 1) * span, :],
            preferred_element_type=jnp.float32,
        ).astype(jnp.bfloat16)
        out_ref[:, g * GROUP : (g + 1) * GROUP, :] = rows.reshape(expert_count, GROUP, inner_width)


def combine_kernel(routes_ref, probs_ref, hidden_ref, *refs, top_count):
    back_refs, (hid_ref, prob_ref) = refs[:-2], refs[-2:]
    span = GROUP * top_count
    inner_width = hidden_ref.shape[1]
    ones = jnp.ones((top_count, inner_width), jnp.bfloat16)
    totals = []
    row = lax.broadcasted_iota(jnp.int32, (top_count, span), 0)
    col = lax.broadcasted_iota(jnp.int32, (top_count, span), 1)
    across = (((0,), (0,)), ((), ()))
    lanes = (((1,), (1,)), ((), ()))
    for g in range(routes_ref.shape[0]):
        chosen = chosen_slots(routes_ref[g : g + 1, :], len(back_refs), top_count)
        pick = jnp.where(chosen, 1.0, 0.0).astype(jnp.bfloat16)
        scaled = jnp.where(chosen, probs_ref[g : g + 1, :].astype(jnp.float32), 0.0)
        block = jnp.concatenate(
            [ref[g * GROUP : (g + 1) * GROUP, :] for ref in back_refs], axis=0
        )
        mine = lax.dot_general(pick, block, across, preferred_element_type=jnp.float32)
        hid_ref[g * span : (g + 1) * span, :] = lax.dot_general(
            scaled.astype(jnp.bfloat16), block, across, preferred_element_type=jnp.float32
        ).astype(jnp.bfloat16)
        product = mine * hidden_ref[g * span : (g + 1) * span, :].astype(jnp.float32)
        part = product[:, :span]
        for first in range(span, inner_width, span):
            part += product[:, first : first + span]
        total = jnp.sum(part.T, axis=0, keepdims=True)
        totals.append(jnp.where(col % top_count == row, total, 0.0).astype(jnp.bfloat16))
    totals = jnp.concatenate(totals, axis=1)
    slot = lax.broadcasted_iota(jnp.int32, (totals.shape[1], prob_ref.shape[1]), 0)
    token = lax.broadcasted_iota(jnp.int32, slot.shape, 1)
    to_token = jnp.where(token == slot // top_count, 1.0, 0.0).astype(jnp.bfloat16)
    prob_ref[...] = jnp.dot(totals, to_token, preferred_element_type=jnp.float32).astype(jnp.bfloat16)


def back_kernel(order_ref, *refs, places, step, block):
    pieces, w_ref = refs[: len(places)], refs[len(places)]
    out_refs, (held, rows_held, sems) = refs[len(places) + 1 : -3], refs[-3:]
    copies = []
    for i, (first, rows) in enumerate(places):
        copies.append(
            pltpu.make_async_copy(pieces[i], held.at[pl.ds(first, rows)], sems.at[i])
        )
        copies[i].start()
    waited = 0
    for first in range(0, held.shape[0], step):
        while waited < len(places) and places[waited][0] < first + step:
            copies[waited].wait()
            waited += 1
        rows = lax.dot_general(
            held[first : first + step, :],
            w_ref[...],
            (((1,), (1,)), ((), ())),
            preferred_element_type=jnp.float32,
        ).astype(jnp.bfloat16)
        for j in range(step // block):
            rows_held[first // block + j] = rows[j * block : (j + 1) * block, :]
    for k, out_ref in enumerate(out_refs):
        out_ref[...] = rows_held[order_ref[k]]


def weight_kernel(ids_ref, *refs, places, first_col):
    hidden_ref, out_ref, held, rows_held, sems, row_sems = refs[-6:]
    pieces = refs[: len(places)]
    block = hidden_ref.shape[1]
    cols = pl.ds(first_col, out_ref.shape[1])
    copies = []
    for j in range(hidden_ref.shape[0]):
        copies.append(
            pltpu.make_async_copy(
                hidden_ref.at[ids_ref[j]], rows_held.at[pl.ds(j * block, block)], row_sems.at[j]
            )
        )
    for i, (first, rows) in enumerate(places):
        copies.append(
            pltpu.make_async_copy(pieces[i].at[:, cols], held.at[pl.ds(first, rows)], sems.at[i])
        )
    for copy in copies:
        copy.start()
    for copy in copies:
        copy.wait()
    tile = min(TILE, out_ref.shape[1])

    @pl.loop(0, out_ref.shape[1] // tile)
    def _(n):
        part = pl.ds(pl.multiple_of(n * tile, tile), tile)
        out_ref[:, part] = lax.dot_general(
            rows_held[...],
            held[:, part],
            (((0,), (0,)), ((), ())),
            preferred_element_type=jnp.float32,
        ).astype(jnp.bfloat16)


def ring_of_chips(chip_count):
    return list(range(0, chip_count, 2)) + list(range(chip_count - 1, 0, -2))


def gather_round(grad_out, peer_count):
    token_count = grad_out.shape[0]
    half = token_count // 2
    chips = peer_count // 2
    ring = ring_of_chips(chips)
    place = {chip: i for i, chip in enumerate(ring)}
    ahead = [
        (2 * chip + core, 2 * ring[(place[chip] + 1) % chips] + core)
        for chip in range(chips)
        for core in range(2)
    ]
    behind = [(b, a) for a, b in ahead]
    swap = [(i, i ^ 1) for i in range(peer_count)]
    low, high = grad_out[:half], grad_out[half:]
    offsets, own_core = [0], [[(low, 0, half), (high, half, half)]]
    low_fore = low_aft = low
    high_fore = high_aft = high
    for s in range(1, chips // 2):
        low_fore = lax.ppermute(low_fore, "expert", ahead)
        high_aft = lax.ppermute(high_aft, "expert", behind)
        high_fore = lax.ppermute(high_fore, "expert", ahead)
        low_aft = lax.ppermute(low_aft, "expert", behind)
        own_core += [
            [(low_fore, 0, half), (high_fore, half, half)],
            [(low_aft, 0, half), (high_aft, half, half)],
        ]
        offsets += [-s, s]
    late = (
        lax.ppermute(low_fore, "expert", ahead),
        lax.ppermute(high_aft, "expert", behind),
        high_fore,
        low_aft,
    )
    own_core.append([(late[0], 0, half), (late[1], half, half)])
    offsets.append(chips // 2)
    pieces, places = [], []
    table = np.zeros((peer_count, peer_count), np.int32)
    for i, parts in enumerate(own_core):
        for j in range(2):
            for array, first, rows in parts:
                pieces.append(lax.ppermute(array, "expert", swap) if j else array)
                places.append(((2 * i + j) * token_count + first, rows))
        for peer in range(peer_count):
            chip, core = peer // 2, peer % 2
            source = ring[(place[chip] + offsets[i]) % chips]
            table[peer, 2 * i] = 2 * source + core
            table[peer, 2 * i + 1] = 2 * source + 1 - core
    return pieces, places, table, late


def exchange(blocks, some):
    peers = range(len(blocks))
    return {k: lax.ppermute(blocks[k], "expert", [(i, i ^ k) for i in peers]) for k in some}


def dense_on_device(grad_out, hidden, routes, probs, w_down):
    token_count, model_width = grad_out.shape
    top_count = routes.shape[1]
    inner_width = hidden.shape[2]
    peer_count = lax.axis_size("expert")
    slot_count = token_count * top_count
    row_count = peer_count * token_count
    span = GROUP * top_count
    me = lax.axis_index("expert")
    route_rows = routes.reshape(slot_count // span, span)
    prob_rows = probs.reshape(slot_count // span, span)
    hidden_rows = hidden.reshape(slot_count, inner_width)
    local_weight = w_down[0]
    params = pltpu.CompilerParams(vmem_limit_bytes=VMEM)
    small = pltpu.CompilerParams(vmem_limit_bytes=SMALL)
    scalars = pl.BlockSpec(memory_space=pltpu.SMEM)
    whole = pl.BlockSpec(memory_space=pltpu.VMEM)
    far = pl.BlockSpec(memory_space=pltpu.HBM)
    block = jax.ShapeDtypeStruct((token_count, inner_width), jnp.bfloat16)

    pieces, places, table, late = gather_round(grad_out, peer_count)
    ids = lax.dynamic_index_in_dim(jnp.asarray(table), me, 0, keepdims=False)
    order = np.stack([np.argsort(table[peer] ^ peer) for peer in range(peer_count)])
    order = lax.dynamic_index_in_dim(
        jnp.asarray(order.astype(np.int32)), me, 0, keepdims=False
    )

    sent = pl.pallas_call(
        functools.partial(dispatch_kernel, expert_count=peer_count, top_count=top_count),
        out_shape=jax.ShapeDtypeStruct((peer_count, token_count, inner_width), jnp.bfloat16),
        in_specs=[whole] * 3,
        out_specs=whole,
        compiler_params=small,
        name="dispatch",
    )(route_rows, prob_rows, hidden_rows)
    sent, _ = lax.optimization_barrier((sent, late))
    got_hidden = lax.all_to_all(sent, "expert", split_axis=0, concat_axis=0, tiled=True)

    back = pl.pallas_call(
        functools.partial(back_kernel, places=places, step=4 * token_count, block=token_count),
        out_shape=[block] * peer_count,
        in_specs=[scalars] + [far] * len(pieces) + [whole],
        out_specs=[whole] * peer_count,
        scratch_shapes=[
            pltpu.VMEM((row_count, model_width), jnp.bfloat16),
            pltpu.VMEM((peer_count, token_count, inner_width), jnp.bfloat16),
            pltpu.SemaphoreType.DMA((len(pieces),)),
        ],
        compiler_params=params,
        cost_estimate=pl.CostEstimate(
            flops=2 * row_count * inner_width * model_width,
            bytes_accessed=2 * (row_count + inner_width) * model_width,
            transcendentals=0,
        ),
        name="back_rows",
    )(order, *pieces, local_weight)
    held_back = range(peer_count - 2, peer_count)
    got_back = {0: back[0]} | exchange(back, [k for k in range(1, peer_count) if k not in held_back])

    near = {k: got_back[k] for k in range(1, peer_count // 2) if k in got_back}
    got_hidden, near = lax.optimization_barrier((got_hidden, near))
    got_back |= near
    width = model_width // SPLIT
    grad_w = [
        pl.pallas_call(
            functools.partial(weight_kernel, places=places, first_col=n * width),
            out_shape=jax.ShapeDtypeStruct((inner_width, width), jnp.bfloat16),
            in_specs=[scalars] + [far] * len(pieces) + [pl.BlockSpec(memory_space=pl.ANY)],
            out_specs=whole,
            scratch_shapes=[
                pltpu.VMEM((row_count, width), jnp.bfloat16),
                pltpu.VMEM((row_count, inner_width), jnp.bfloat16),
                pltpu.SemaphoreType.DMA((len(pieces),)),
                pltpu.SemaphoreType.DMA((peer_count,)),
            ],
            compiler_params=params,
            cost_estimate=pl.CostEstimate(
                flops=2 * row_count * inner_width * width,
                bytes_accessed=2 * (row_count * (width + inner_width) + inner_width * width),
                transcendentals=0,
            ),
            name="grad_w",
        )(ids, *pieces, got_hidden)
        for n in range(SPLIT)
    ]
    grad_w = jnp.concatenate(grad_w, axis=1) if SPLIT > 1 else grad_w[0]

    back, grad_w = lax.optimization_barrier((back, grad_w))
    got_back |= exchange(back, held_back)
    got_back = [got_back[k] for k in range(peer_count)]
    grad_hidden, grad_probs = pl.pallas_call(
        functools.partial(combine_kernel, top_count=top_count),
        out_shape=(
            jax.ShapeDtypeStruct((slot_count, inner_width), jnp.bfloat16),
            jax.ShapeDtypeStruct((top_count, token_count), jnp.bfloat16),
        ),
        in_specs=[whole] * (3 + peer_count),
        out_specs=(whole, whole),
        compiler_params=small,
        name="combine",
    )((routes ^ me).reshape(slot_count // span, span), prob_rows, hidden_rows, *got_back)
    return (
        grad_hidden.reshape(token_count, top_count, inner_width),
        grad_probs.T,
        grad_w[None],
    )


def on_device(grad_out, hidden, routes, probs, w_down):
    token_count = grad_out.shape[0]
    top_count = routes.shape[1]
    peer_count = lax.axis_size("expert")
    dense = (
        2 * top_count >= peer_count
        and lax.axis_size("dp") == 1
        and peer_count % 4 == 0
        and peer_count & (peer_count - 1) == 0
        and token_count % (2 * GROUP) == 0
        and GROUP * top_count == 128
        and hidden.shape[2] % 128 == 0
    )
    body = dense_on_device if dense else padded_on_device
    return body(grad_out, hidden, routes, probs, w_down)


def solution(mesh):
    in_specs = (
        P(("groups", "expert", "dp"), None),
        P(("groups", "expert", "dp"), None, None),
        P(("groups", "expert", "dp"), None),
        P(("groups", "expert", "dp"), None),
        P("expert", "dp", None),
    )
    out_specs = (
        P(("groups", "expert", "dp"), None, None),
        P(("groups", "expert", "dp"), None),
        P(("groups", "expert"), "dp", None),
    )
    return jax.shard_map(
        on_device, mesh=mesh, in_specs=in_specs, out_specs=out_specs, check_vma=False
    )
```
